32 devices in a mesh: freq: 16 (over z, y, x), src: 2 (over core).
Axes of the slice: x: 2, y: 2, z: 4, core: 2. Of those that a mesh axis runs over, the one named last changes fastest.
Arguments:
- samples: bfloat16 [128, 2048, 128], P('freq', None, 'src'), may hold values from -6 to 6
- initial_offset: float32 [2, 1024, 128, 128], P(None, 'freq'), may hold values from -0.875 to 0.875
Outputs:
- demixing: float32 [2, 1024, 128, 128], P(None, 'freq', 'src')
- source_power: float32 [128, 128], P('src')
The draws below stay inside these ranges and needn't reach their ends.
All inputs are finite; a program needn't handle non-finite values.
Results may differ from the reference program's by a relative error of at most 0.0051.
Values may be sent and summed in bfloat16 or wider, within the bound.
A program may use at most 128 MiB of HBM per device.

```python
import jax
import jax.numpy as jnp
from jax import lax

K = 128
FRAME_LEN = 2048
ITERS = 3
BINS = 1024
FRAMES = 128


def steps_of(key, extent, split, smallest, top_value):
    gain = 1.0
    for position, parts in split:
        draws = jax.random.uniform(jax.random.fold_in(jax.random.fold_in(key, 6), position), (parts,), jnp.float32, smallest / len(split), top_value / len(split))
        gain = gain * jnp.repeat(jnp.exp(draws), extent[position] // parts).reshape((-1,) + (1,) * (len(extent) - 1 - position))
    return gain


def gaussian(key, shape, scale, limit, shards=(), kind=jnp.bfloat16):
    drawn = scale * jax.random.normal(key, shape, jnp.float32)
    if shards:
        drawn = drawn * steps_of(key, shape, shards, -0.22, 0.18)
    return jnp.clip(drawn, -limit, limit).astype(kind)


def setup_inputs(seed: int = 0) -> dict:
    key_list = jax.random.split(jax.random.key(seed), 3)
    return {
        "samples": gaussian(key_list[0], (FRAMES, FRAME_LEN, K), 1.0, 6.0, ((0, 16), (2, 2))),
        "initial_offset": gaussian(key_list[1], (2, BINS, K, K), (0.7 / K ** 0.5), 0.875, ((1, 16),), jnp.float32),
    }


step_size = 0.3
epsilon = 1e-06

def dft_table(length):
    sample_idx = jnp.arange(length, dtype=jnp.int32)
    bin_idx = jnp.arange(length // 2, dtype=jnp.int32)
    phase = (sample_idx[:, None] * bin_idx[None, :] % length).astype(jnp.float32) * (2.0 * jnp.pi / length)
    window = (0.5 - 0.5 * jnp.cos(sample_idx.astype(jnp.float32) * (2.0 * jnp.pi / length))) * jnp.sqrt(jnp.float32(8.0 / (3.0 * length)))
    return jnp.concatenate([window[:, None] * jnp.cos(phase), -window[:, None] * jnp.sin(phase)], axis=1).astype(jnp.bfloat16)

def batched(left, right, form):
    return jnp.einsum(form, left, right, precision=lax.Precision.HIGHEST)

def demix_rows(w_real, w_imag, x_real, x_imag):
    form = 'bkm,bmt->bkt'
    y_real = batched(w_real, x_real, form) - batched(w_imag, x_imag, form)
    y_imag = batched(w_real, x_imag, form) + batched(w_imag, x_real, form)
    return (y_real, y_imag)

def update_rows(w_real, w_imag, own_real, own_imag, y_real, y_imag, all_real, all_imag, source_power, identity_rows):
    frames = y_real.shape[2]
    phi_real = y_real / source_power
    phi_imag = y_imag / source_power
    form = 'bkt,bjt->bkj'
    gram_real = (batched(phi_real, all_real, form) + batched(phi_imag, all_imag, form)) / frames
    gram_imag = (batched(phi_imag, all_real, form) - batched(phi_real, all_imag, form)) / frames
    diff_real = identity_rows - gram_real
    diff_imag = -gram_imag
    other = 'bkj,bjm->bkm'
    new_real = own_real + step_size * (batched(diff_real, w_real, other) - batched(diff_imag, w_imag, other))
    new_imag = own_imag + step_size * (batched(diff_real, w_imag, other) + batched(diff_imag, w_real, other))
    return (new_real, new_imag)

def reference(samples, initial_offset):
    spectra = jnp.einsum('fnm,nc->fmc', samples.astype(jnp.float32), dft_table(FRAME_LEN).astype(jnp.float32)).astype(jnp.bfloat16)
    spectra = spectra.reshape(FRAMES, K, 2, BINS)
    x_real = jnp.transpose(spectra[:, :, 0, :], (2, 1, 0)).astype(jnp.float32)
    x_imag = jnp.transpose(spectra[:, :, 1, :], (2, 1, 0)).astype(jnp.float32)
    identity = jnp.eye(K, dtype=jnp.float32)
    w_real = initial_offset[0] + identity
    w_imag = initial_offset[1]
    source_power = jnp.zeros((K, FRAMES), jnp.float32)
    for sweep in range(ITERS):
        y_real, y_imag = demix_rows(w_real, w_imag, x_real, x_imag)
        rounded = lax.optimization_barrier(jnp.stack([y_real, y_imag]).astype(jnp.bfloat16))
        values = rounded.astype(jnp.float32)
        bin_sums = lax.optimization_barrier(jnp.sum(values[0] * values[0] + values[1] * values[1], axis=0))
        source_power = jnp.sqrt(bin_sums / BINS + epsilon)
        w_real, w_imag = update_rows(w_real, w_imag, w_real, w_imag, values[0], values[1], values[0], values[1], source_power, identity)
    return (jnp.stack([w_real, w_imag]), source_power)
```

```python
import functools

import jax
import jax.numpy as jnp
from jax import lax
from jax.experimental import pallas as pl
from jax.experimental.pallas import tpu as pltpu
from jax.sharding import PartitionSpec as P

ITERS = 3

step_size = 0.3
epsilon = 1e-06
MESH = pl.DeviceIdType.MESH
LOW_STEPS = 64


def waves(count, stride, length):
    index = jnp.arange(count, dtype=jnp.int32) * stride
    bin_idx = jnp.arange(length // 2, dtype=jnp.int32)
    phase = (index[:, None] * bin_idx[None, :] % length).astype(jnp.float32) * (
        2.0 * jnp.pi / length
    )
    return lax.optimization_barrier((jnp.cos(phase), jnp.sin(phase)))


def dft_table(length):
    high_cos, high_sin = waves(length // LOW_STEPS, LOW_STEPS, length)
    low_cos, low_sin = waves(LOW_STEPS, 1, length)
    sample_idx = jnp.arange(length, dtype=jnp.int32)
    window = (
        0.5 - 0.5 * jnp.cos(sample_idx.astype(jnp.float32) * (2.0 * jnp.pi / length))
    ) * jnp.sqrt(jnp.float32(8.0 / (3.0 * length)))
    window = lax.optimization_barrier(window).reshape(-1, LOW_STEPS, 1)
    a_cos, a_sin = high_cos[:, None, :], high_sin[:, None, :]
    b_cos, b_sin = low_cos[None], low_sin[None]
    cos_part = (window * (a_cos * b_cos - a_sin * b_sin)).astype(jnp.bfloat16)
    sin_part = (-window * (a_sin * b_cos + a_cos * b_sin)).astype(jnp.bfloat16)
    return jnp.concatenate([cos_part, sin_part], axis=2).reshape(length, length)


def halves(value):
    high = value.astype(jnp.bfloat16)
    low = (value - high.astype(jnp.float32)).astype(jnp.bfloat16)
    return high, low


def dot_nn(left, right):
    return lax.dot_general(left, right, (((1,), (0,)), ((), ())), preferred_element_type=jnp.float32)


def dot_nt(left, right):
    return lax.dot_general(left, right, (((1,), (1,)), ((), ())), preferred_element_type=jnp.float32)


def block_pair(real_imag, width):
    swapped = jnp.concatenate([-real_imag[:, width:], real_imag[:, :width]], axis=1)
    return jnp.concatenate([real_imag, swapped], axis=0)


def demix_kernel(
    dims,
    x_ref,
    offset_ref,
    out_ref,
    power_ref,
    stage,
    w_buf,
    x_buf,
    y_buf,
    sums,
    power,
    parts,
    received,
    gathered,
    load_sem,
    send_sem,
    recv_sem,
    last_sem,
):
    freq_devices, src_devices, total_bins = dims
    devices = freq_devices * src_devices
    my_freq, my_src = lax.axis_index("freq"), lax.axis_index("src")
    me = my_freq * src_devices + my_src
    bins, frames, width = x_ref.shape[1], x_ref.shape[2], x_ref.shape[3]
    rows = width // src_devices
    chunk = width // devices

    def place(index):
        return (index // src_devices, lax.rem(index, src_devices))

    load = pltpu.make_async_copy(
        offset_ref.at[:, pl.ds(my_src * bins, bins)], stage, load_sem
    )
    load.start()

    barrier = pltpu.get_barrier_semaphore()

    def greet(step, carry):
        pl.semaphore_signal(
            barrier, inc=1, device_id=place(lax.rem(me + step, devices)), device_id_type=MESH
        )
        return carry

    lax.fori_loop(1, devices, greet, 0)
    load.wait()
    row_id = lax.broadcasted_iota(jnp.int32, (width, 2 * width), 0)
    col_id = lax.broadcasted_iota(jnp.int32, (width, 2 * width), 1)
    identity = jnp.where(row_id == col_id, 1.0, 0.0).astype(jnp.float32)

    def separate(b, w):
        high, low = halves(w)
        product = dot_nt(jnp.concatenate([high, low], axis=0), x_buf[b])
        y = (product[:width] + product[width:]).astype(jnp.bfloat16)
        y_buf[b] = y
        values = y.astype(jnp.float32)
        squares = values * values
        sums[...] += squares[:, :frames] + squares[:, frames:]

    def first(b, carry):
        w = jnp.concatenate([stage[0, b], stage[1, b]], axis=1) + identity
        w_buf[b] = w
        x_real, x_imag = x_ref[0, b], x_ref[1, b]
        upper = jnp.concatenate([x_real, -x_imag], axis=1)
        lower = jnp.concatenate([x_imag, x_real], axis=1)
        x_buf[b] = jnp.concatenate([upper, lower], axis=0)
        separate(b, w)
        return carry

    def improved(b, scale):
        y = y_buf[b]
        high, low = halves(y.astype(jnp.float32) * scale)
        product = dot_nt(jnp.concatenate([high, low], axis=0), block_pair(y, frames))
        diff = identity - (product[:width] + product[width:])
        d_high, d_low = halves(diff)
        w = w_buf[b]
        w_high, w_low = halves(w)
        change = dot_nn(jnp.concatenate([d_high, d_low], axis=0), block_pair(w_high, width))
        change_low = dot_nn(d_high, block_pair(w_low, width))
        return w + step_size * (change[:width] + change[width:] + change_low)

    def add_up(sweep):
        total = sums[...]
        for owner in range(devices):
            parts[owner] = total[owner * chunk : (owner + 1) * chunk]

        def scatter(step, carry):
            owner = lax.rem(me + step, devices)
            pltpu.make_async_remote_copy(
                src_ref=parts.at[owner],
                dst_ref=received.at[sweep, step - 1],
                send_sem=send_sem.at[sweep, 0],
                recv_sem=recv_sem.at[sweep, 0],
                device_id=place(owner),
                device_id_type=MESH,
            ).start()
            return carry

        lax.fori_loop(1, devices, scatter, 0)
        pltpu.make_async_copy(
            received.at[sweep], received.at[sweep], recv_sem.at[sweep, 0]
        ).wait()
        mine = parts[me] + jnp.sum(received[sweep], axis=0)
        gathered[sweep, me] = jnp.sqrt(mine / total_bins + epsilon)

        def spread(step, carry):
            pltpu.make_async_remote_copy(
                src_ref=gathered.at[sweep, me],
                dst_ref=gathered.at[sweep, me],
                send_sem=send_sem.at[sweep, 1],
                recv_sem=recv_sem.at[sweep, 1],
                device_id=place(lax.rem(me + step, devices)),
                device_id_type=MESH,
            ).start()
            return carry

        lax.fori_loop(1, devices, spread, 0)
        for phase in range(2):
            pltpu.make_async_copy(
                received.at[sweep], received.at[sweep], send_sem.at[sweep, phase]
            ).wait()
        pltpu.make_async_copy(
            received.at[sweep], received.at[sweep], recv_sem.at[sweep, 1]
        ).wait()
        for owner in range(devices):
            power[owner * chunk : (owner + 1) * chunk] = gathered[sweep, owner]
        inverse = 1.0 / (power[...] * frames)
        return jnp.concatenate([inverse, inverse], axis=1)

    sums[...] = jnp.zeros_like(sums)
    lax.fori_loop(0, bins, first, 0)
    pl.semaphore_wait(barrier, devices - 1)

    for sweep in range(ITERS - 1):
        scale = add_up(sweep)
        sums[...] = jnp.zeros_like(sums)

        def again(b, carry, scale=scale):
            w = improved(b, scale)
            w_buf[b] = w
            separate(b, w)
            return carry

        lax.fori_loop(0, bins, again, 0)

    scale = add_up(ITERS - 1)
    power_ref[...] = power[pl.ds(pl.multiple_of(my_src * rows, rows), rows), :]

    def last(b, carry):
        w = improved(b, scale)
        stage[0, b] = w[:, :width]
        stage[1, b] = w[:, width:]
        return carry

    lax.fori_loop(0, bins, last, 0)
    here = pl.ds(my_src * bins, bins)
    keep = pltpu.make_async_copy(
        stage.at[:, :, pl.ds(pl.multiple_of(my_src * rows, rows), rows)],
        out_ref.at[:, here],
        load_sem,
    )
    keep.start()
    other = 1 - my_src
    give = pltpu.make_async_remote_copy(
        src_ref=stage.at[:, :, pl.ds(pl.multiple_of(other * rows, rows), rows)],
        dst_ref=out_ref.at[:, here],
        send_sem=last_sem.at[0],
        recv_sem=last_sem.at[1],
        device_id=(my_freq, other),
        device_id_type=MESH,
    )
    give.start()
    keep.wait()
    give.wait()


def shards(samples, initial_offset):
    freq_devices = lax.axis_size("freq")
    src_devices = lax.axis_size("src")
    devices = freq_devices * src_devices
    frames_here, length, mics_here = samples.shape
    bin_count = length // 2
    pair_bins = initial_offset.shape[1]
    bins = pair_bins // src_devices
    width = initial_offset.shape[2]
    frame_total = frames_here * freq_devices
    chunk = width // devices
    spectra = jnp.einsum(
        "fnm,nc->cfm", samples, dft_table(length), preferred_element_type=jnp.float32
    ).astype(jnp.bfloat16)
    spectra = spectra.reshape(2, bin_count, frames_here * mics_here)
    regrouped = lax.all_to_all(
        spectra, ("freq", "src"), split_axis=1, concat_axis=2, tiled=True
    )
    regrouped = regrouped.reshape(
        2, bins, freq_devices, src_devices, frames_here, mics_here
    )
    x = jnp.transpose(regrouped, (0, 1, 2, 4, 3, 5)).reshape(2, bins, frame_total, width)
    f32, bf16 = jnp.float32, jnp.bfloat16
    return pl.pallas_call(
        functools.partial(demix_kernel, (freq_devices, src_devices, bin_count)),
        out_shape=(
            jax.ShapeDtypeStruct((2, pair_bins, width // src_devices, width), f32),
            jax.ShapeDtypeStruct((width // src_devices, frame_total), f32),
        ),
        in_specs=[
            pl.BlockSpec(memory_space=pltpu.VMEM),
            pl.BlockSpec(memory_space=pl.ANY),
        ],
        out_specs=(
            pl.BlockSpec(memory_space=pl.ANY),
            pl.BlockSpec(memory_space=pltpu.VMEM),
        ),
        scratch_shapes=[
            pltpu.VMEM((2, bins, width, width), f32),
            pltpu.VMEM((bins, width, 2 * width), f32),
            pltpu.VMEM((bins, 2 * frame_total, 2 * width), bf16),
            pltpu.VMEM((bins, width, 2 * frame_total), bf16),
            pltpu.VMEM((width, frame_total), f32),
            pltpu.VMEM((width, frame_total), f32),
            pltpu.VMEM((devices, chunk, frame_total), f32),
            pltpu.VMEM((ITERS, devices - 1, chunk, frame_total), f32),
            pltpu.VMEM((ITERS, devices, chunk, frame_total), f32),
            pltpu.SemaphoreType.DMA,
            pltpu.SemaphoreType.DMA((ITERS, 2)),
            pltpu.SemaphoreType.DMA((ITERS, 2)),
            pltpu.SemaphoreType.DMA((2,)),
        ],
        compiler_params=pltpu.CompilerParams(
            collective_id=0, has_side_effects=True, vmem_limit_bytes=48 * 1024 * 1024
        ),
    )(x, initial_offset)


def solution(mesh):
    in_specs = (P("freq", None, "src"), P(None, "freq", None, None))
    out_specs = (P(None, "freq", "src", None), P("src", None))
    return jax.shard_map(shards, mesh=mesh, in_specs=in_specs, out_specs=out_specs, check_vma=False)
```

```python
import functools

import jax
import jax.numpy as jnp
from jax import lax
from jax.experimental import pallas as pl
from jax.experimental.pallas import tpu as pltpu
from jax.sharding import PartitionSpec as P

ITERS = 3

step_size = 0.3
epsilon = 1e-06
MESH = pl.DeviceIdType.MESH
LOW_STEPS = 128
GROUP_BINS = 128
PAIR = 2


def waves(bin_idx, count, stride, length):
    index = jnp.arange(count, dtype=jnp.int32) * stride
    phase = (bin_idx[:, None] * index[None, :] % length).astype(jnp.float32) * (
        2.0 * jnp.pi / length
    )
    return jnp.cos(phase), jnp.sin(phase)


def window_of(length):
    sample_idx = jnp.arange(length, dtype=jnp.int32)
    return (
        0.5 - 0.5 * jnp.cos(sample_idx.astype(jnp.float32) * (2.0 * jnp.pi / length))
    ) * jnp.sqrt(jnp.float32(8.0 / (3.0 * length)))


def halves(value):
    high = value.astype(jnp.bfloat16)
    low = (value - high.astype(jnp.float32)).astype(jnp.bfloat16)
    return high, low


def dot_nn(left, right):
    return lax.dot_general(left, right, (((1,), (0,)), ((), ())), preferred_element_type=jnp.float32)


def dot_nt(left, right):
    return lax.dot_general(left, right, (((1,), (1,)), ((), ())), preferred_element_type=jnp.float32)


def block_pair(real_imag, width):
    swapped = jnp.concatenate([-real_imag[:, width:], real_imag[:, :width]], axis=1)
    return jnp.concatenate([real_imag, swapped], axis=0)


def spectra_kernel(
    dims,
    s_ref,
    high_cos,
    high_sin,
    low_cos,
    low_sin,
    window,
    out_ref,
    table,
    send_buf,
    keep_sem,
    send_sem,
    recv_sem,
):
    freq_devices, src_devices = dims
    devices = freq_devices * src_devices
    my_freq, my_src = lax.axis_index("freq"), lax.axis_index("src")
    slot = my_src * freq_devices + my_freq
    bins = out_ref.shape[2]
    length = s_ref.shape[1]
    members = GROUP_BINS // bins
    groups = devices // members

    def place(index):
        return (lax.rem(index, freq_devices), index // freq_devices)

    barrier = pltpu.get_barrier_semaphore()

    def greet(step, carry):
        pl.semaphore_signal(
            barrier, inc=1, device_id=place(lax.rem(slot + step, devices)), device_id_type=MESH
        )
        return carry

    lax.fori_loop(1, devices, greet, 0)

    def group_of(step):
        return lax.rem(slot // members + step, groups)

    def compute(step):
        group = group_of(step)
        rows = pl.ds(pl.multiple_of(group * GROUP_BINS, GROUP_BINS), GROUP_BINS)
        l_cos, l_sin = low_cos[rows, :], low_sin[rows, :]
        h_cos, h_sin = high_cos[rows, :], high_sin[rows, :]
        for high in range(length // LOW_STEPS):
            columns = slice(high * LOW_STEPS, (high + 1) * LOW_STEPS)
            a_cos, a_sin = h_cos[:, high : high + 1], h_sin[:, high : high + 1]
            weight = window[:, columns]
            table[:GROUP_BINS, columns] = (weight * (a_cos * l_cos - a_sin * l_sin)).astype(
                jnp.bfloat16
            )
            table[GROUP_BINS:, columns] = (-weight * (a_sin * l_cos + a_cos * l_sin)).astype(
                jnp.bfloat16
            )
        y = dot_nt(table[...], s_ref[...]).astype(jnp.bfloat16)
        for member in range(members):
            owner = group * members + member
            send_buf[owner, 0] = y[member * bins : (member + 1) * bins]
            send_buf[owner, 1] = y[GROUP_BINS + member * bins : GROUP_BINS + (member + 1) * bins]

    def send(step):
        for member in range(members):
            owner = group_of(step) * members + lax.rem(slot + member, members)

            @pl.when(owner == slot)
            def _():
                pltpu.make_async_copy(send_buf.at[owner], out_ref.at[slot], keep_sem).start()

            @pl.when(owner != slot)
            def _():
                pltpu.make_async_remote_copy(
                    src_ref=send_buf.at[owner],
                    dst_ref=out_ref.at[slot],
                    send_sem=send_sem,
                    recv_sem=recv_sem,
                    device_id=place(owner),
                    device_id_type=MESH,
                ).start()

    compute(0)
    pl.semaphore_wait(barrier, devices - 1)
    send(0)

    def body(step, carry):
        compute(step)
        send(step)
        return carry

    lax.fori_loop(1, groups, body, 0)
    pltpu.make_async_copy(send_buf.at[slot], out_ref.at[slot], keep_sem).wait()
    others = out_ref.at[pl.ds(0, devices - 1)]
    pltpu.make_async_copy(others, others, send_sem).wait()
    pltpu.make_async_copy(others, others, recv_sem).wait()


def demix_kernel(
    dims,
    x_ref,
    offset_ref,
    out_ref,
    power_ref,
    stage,
    w_buf,
    x_buf,
    y_buf,
    sums,
    power,
    parts,
    received,
    gathered,
    load_sem,
    send_sem,
    recv_sem,
    last_sem,
):
    freq_devices, src_devices, total_bins, frames_here = dims
    devices = freq_devices * src_devices
    my_freq, my_src = lax.axis_index("freq"), lax.axis_index("src")
    me = my_freq * src_devices + my_src
    bins = x_ref.shape[1]
    width = offset_ref.shape[2]
    frames = frames_here * freq_devices
    rows = width // src_devices
    chunk = width // devices

    def place(index):
        return (index // src_devices, lax.rem(index, src_devices))

    load = pltpu.make_async_copy(
        offset_ref.at[:, pl.ds(my_src * bins, bins)], stage, load_sem
    )
    load.start()

    barrier = pltpu.get_barrier_semaphore()

    def greet(step, carry):
        pl.semaphore_signal(
            barrier, inc=1, device_id=place(lax.rem(me + step, devices)), device_id_type=MESH
        )
        return carry

    lax.fori_loop(1, devices, greet, 0)
    load.wait()
    row_id = lax.broadcasted_iota(jnp.int32, (width, 2 * width), 0)
    col_id = lax.broadcasted_iota(jnp.int32, (width, 2 * width), 1)
    identity = jnp.where(row_id == col_id, 1.0, 0.0).astype(jnp.float32)

    def separate(first_bin, w_list, x_list):
        products = []
        for w, x in zip(w_list, x_list):
            high, low = halves(w)
            products.append(dot_nt(jnp.concatenate([high, low], axis=0), x))
        y_list = [(p[:width] + p[width:]).astype(jnp.bfloat16) for p in products]
        squares = 0.0
        for y in y_list:
            values = y.astype(jnp.float32)
            squares = squares + values * values
        for k in range(PAIR):
            w_buf[first_bin + k] = w_list[k]
            y_buf[first_bin + k] = y_list[k]
        sums[...] += squares[:, :frames] + squares[:, frames:]

    def gather_frames(part):
        pieces = [part[k * freq_devices : (k + 1) * freq_devices] for k in range(src_devices)]
        return jnp.concatenate(
            [
                jnp.concatenate([p[:, f * rows : (f + 1) * rows] for p in pieces], axis=1)
                for f in range(frames_here)
            ],
            axis=0,
        )

    def first(step, carry):
        b = step * PAIR
        w_list, x_list = [], []
        for k in range(PAIR):
            w_list.append(jnp.concatenate([stage[0, b + k], stage[1, b + k]], axis=1) + identity)
            x_real, x_imag = gather_frames(x_ref[0, b + k]), gather_frames(x_ref[1, b + k])
            upper = jnp.concatenate([x_real, -x_imag], axis=1)
            lower = jnp.concatenate([x_imag, x_real], axis=1)
            x_list.append(jnp.concatenate([upper, lower], axis=0))
        for k in range(PAIR):
            x_buf[b + k] = x_list[k]
        separate(b, w_list, x_list)
        return carry

    def improved(first_bin, scale):
        y_list = [y_buf[first_bin + k] for k in range(PAIR)]
        w_list = [w_buf[first_bin + k] for k in range(PAIR)]
        diffs = []
        for y in y_list:
            high, low = halves(y.astype(jnp.float32) * scale)
            product = dot_nt(jnp.concatenate([high, low], axis=0), block_pair(y, frames))
            diffs.append(identity - (product[:width] + product[width:]))
        result = []
        for diff, w in zip(diffs, w_list):
            d_high, d_low = halves(diff)
            w_high, w_low = halves(w)
            change = dot_nn(jnp.concatenate([d_high, d_low], axis=0), block_pair(w_high, width))
            change_low = dot_nn(d_high, block_pair(w_low, width))
            result.append(w + step_size * (change[:width] + change[width:] + change_low))
        return result

    def add_up(sweep):
        total = sums[...]
        for owner in range(devices):
            parts[owner] = total[owner * chunk : (owner + 1) * chunk]

        def scatter(step, carry):
            owner = lax.rem(me + step, devices)
            pltpu.make_async_remote_copy(
                src_ref=parts.at[owner],
                dst_ref=received.at[sweep, step - 1],
                send_sem=send_sem.at[sweep, 0],
                recv_sem=recv_sem.at[sweep, 0],
                device_id=place(owner),
                device_id_type=MESH,
            ).start()
            return carry

        lax.fori_loop(1, devices, scatter, 0)
        pltpu.make_async_copy(
            received.at[sweep], received.at[sweep], recv_sem.at[sweep, 0]
        ).wait()
        mine = parts[me] + jnp.sum(received[sweep], axis=0)
        gathered[sweep, me] = jnp.sqrt(mine / total_bins + epsilon)

        def spread(step, carry):
            pltpu.make_async_remote_copy(
                src_ref=gathered.at[sweep, me],
                dst_ref=gathered.at[sweep, me],
                send_sem=send_sem.at[sweep, 1],
                recv_sem=recv_sem.at[sweep, 1],
                device_id=place(lax.rem(me + step, devices)),
                device_id_type=MESH,
            ).start()
            return carry

        lax.fori_loop(1, devices, spread, 0)
        for phase in range(2):
            pltpu.make_async_copy(
                received.at[sweep], received.at[sweep], send_sem.at[sweep, phase]
            ).wait()
        pltpu.make_async_copy(
            received.at[sweep], received.at[sweep], recv_sem.at[sweep, 1]
        ).wait()
        for owner in range(devices):
            power[owner * chunk : (owner + 1) * chunk] = gathered[sweep, owner]
        inverse = 1.0 / (power[...] * frames)
        return jnp.concatenate([inverse, inverse], axis=1)

    sums[...] = jnp.zeros_like(sums)
    lax.fori_loop(0, bins // PAIR, first, 0)
    pl.semaphore_wait(barrier, devices - 1)

    for sweep in range(ITERS - 1):
        scale = add_up(sweep)
        sums[...] = jnp.zeros_like(sums)

        def again(step, carry, scale=scale):
            b = step * PAIR
            x_list = [x_buf[b + k] for k in range(PAIR)]
            separate(b, improved(b, scale), x_list)
            return carry

        lax.fori_loop(0, bins // PAIR, again, 0)

    scale = add_up(ITERS - 1)
    power_ref[...] = power[pl.ds(pl.multiple_of(my_src * rows, rows), rows), :]

    other = 1 - my_src
    own_rows = pl.ds(pl.multiple_of(my_src * rows, rows), rows)
    other_rows = pl.ds(pl.multiple_of(other * rows, rows), rows)

    def keep_copy(start, count):
        return pltpu.make_async_copy(
            stage.at[:, pl.ds(start, count), own_rows],
            out_ref.at[:, pl.ds(my_src * bins + start, count)],
            load_sem,
        )

    def give_copy(start, count):
        return pltpu.make_async_remote_copy(
            src_ref=stage.at[:, pl.ds(start, count), other_rows],
            dst_ref=out_ref.at[:, pl.ds(my_src * bins + start, count)],
            send_sem=last_sem.at[0],
            recv_sem=last_sem.at[1],
            device_id=(my_freq, other),
            device_id_type=MESH,
        )

    def last(step, carry):
        b = step * PAIR
        w_list = improved(b, scale)
        for k in range(PAIR):
            stage[0, b + k] = w_list[k][:, :width]
            stage[1, b + k] = w_list[k][:, width:]
        give_copy(b, PAIR).start()
        keep_copy(b, PAIR).start()
        return carry

    lax.fori_loop(0, bins // PAIR, last, 0)
    keep_copy(0, bins).wait()
    give_copy(0, bins).wait()


def shards(samples, initial_offset):
    freq_devices = lax.axis_size("freq")
    src_devices = lax.axis_size("src")
    devices = freq_devices * src_devices
    frames_here, length, mics_here = samples.shape
    bin_count = length // 2
    pair_bins = initial_offset.shape[1]
    bins = pair_bins // src_devices
    width = initial_offset.shape[2]
    frame_total = frames_here * freq_devices
    chunk = width // devices
    f32, bf16 = jnp.float32, jnp.bfloat16
    row = jnp.arange(bin_count, dtype=jnp.int32)
    bin_idx = (
        row // bins % freq_devices * pair_bins
        + row // (bins * freq_devices) * bins
        + row % bins
    )
    high_cos, high_sin = waves(bin_idx, length // LOW_STEPS, LOW_STEPS, length)
    low_cos, low_sin = waves(bin_idx, LOW_STEPS, 1, length)
    columns = frames_here * mics_here
    frames_of = jnp.transpose(samples, (0, 2, 1)).reshape(columns, length)
    vmem = pl.BlockSpec(memory_space=pltpu.VMEM)
    spectra = pl.pallas_call(
        functools.partial(spectra_kernel, (freq_devices, src_devices)),
        out_shape=jax.ShapeDtypeStruct((devices, 2, bins, columns), bf16),
        in_specs=[vmem] * 6,
        out_specs=vmem,
        scratch_shapes=[
            pltpu.VMEM((2 * GROUP_BINS, length), bf16),
            pltpu.VMEM((devices, 2, bins, columns), bf16),
            pltpu.SemaphoreType.DMA,
            pltpu.SemaphoreType.DMA,
            pltpu.SemaphoreType.DMA,
        ],
        compiler_params=pltpu.CompilerParams(
            collective_id=1, has_side_effects=True, vmem_limit_bytes=40 * 1024 * 1024
        ),
    )(frames_of, high_cos, high_sin, low_cos, low_sin, window_of(length)[None])
    x = jnp.transpose(spectra, (1, 2, 0, 3))
    demixing, power = pl.pallas_call(
        functools.partial(demix_kernel, (freq_devices, src_devices, bin_count, frames_here)),
        out_shape=(
            jax.ShapeDtypeStruct((2, pair_bins, width // src_devices, width), f32),
            jax.ShapeDtypeStruct((width // src_devices, frame_total), f32),
        ),
        in_specs=[
            pl.BlockSpec(memory_space=pltpu.VMEM),
            pl.BlockSpec(memory_space=pl.ANY),
        ],
        out_specs=(
            pl.BlockSpec(memory_space=pl.ANY),
            pl.BlockSpec(memory_space=pltpu.VMEM),
        ),
        scratch_shapes=[
            pltpu.VMEM((2, bins, width, width), f32),
            pltpu.VMEM((bins, width, 2 * width), f32),
            pltpu.VMEM((bins, 2 * frame_total, 2 * width), bf16),
            pltpu.VMEM((bins, width, 2 * frame_total), bf16),
            pltpu.VMEM((width, frame_total), f32),
            pltpu.VMEM((width, frame_total), f32),
            pltpu.VMEM((devices, chunk, frame_total), f32),
            pltpu.VMEM((ITERS, devices - 1, chunk, frame_total), f32),
            pltpu.VMEM((ITERS, devices, chunk, frame_total), f32),
            pltpu.SemaphoreType.DMA,
            pltpu.SemaphoreType.DMA((ITERS, 2)),
            pltpu.SemaphoreType.DMA((ITERS, 2)),
            pltpu.SemaphoreType.DMA((2,)),
        ],
        compiler_params=pltpu.CompilerParams(
            collective_id=0, has_side_effects=True, vmem_limit_bytes=48 * 1024 * 1024
        ),
    )(x, initial_offset)
    power = jnp.transpose(power.reshape(-1, frames_here, freq_devices), (0, 2, 1))
    return demixing, power.reshape(-1, frame_total)


def solution(mesh):
    in_specs = (P("freq", None, "src"), P(None, "freq", None, None))
    out_specs = (P(None, "freq", "src", None), P("src", None))
    return jax.shard_map(shards, mesh=mesh, in_specs=in_specs, out_specs=out_specs, check_vma=False)
```

```python
import functools

import jax
import jax.numpy as jnp
from jax import lax
from jax.experimental import pallas as pl
from jax.experimental.pallas import tpu as pltpu
from jax.sharding import PartitionSpec as P

ITERS = 3

step_size = 0.3
epsilon = 1e-06
MESH = pl.DeviceIdType.MESH
LOW_STEPS = 128
GROUP_BINS = 128
PAIR = 8


def waves(bin_idx, count, stride, length):
    index = jnp.arange(count, dtype=jnp.int32) * stride
    phase = (bin_idx[:, None] * index[None, :] % length).astype(jnp.float32) * (
        2.0 * jnp.pi / length
    )
    return jnp.cos(phase), jnp.sin(phase)


def window_of(length):
    sample_idx = jnp.arange(length, dtype=jnp.int32)
    return (
        0.5 - 0.5 * jnp.cos(sample_idx.astype(jnp.float32) * (2.0 * jnp.pi / length))
    ) * jnp.sqrt(jnp.float32(8.0 / (3.0 * length)))


def halves(value):
    high = value.astype(jnp.bfloat16)
    low = (value - high.astype(jnp.float32)).astype(jnp.bfloat16)
    return high, low


def dot_nn(left, right):
    return lax.dot_general(left, right, (((1,), (0,)), ((), ())), preferred_element_type=jnp.float32)


def dot_nt(left, right):
    return lax.dot_general(left, right, (((1,), (1,)), ((), ())), preferred_element_type=jnp.float32)


def block_pair(real_imag, width):
    swapped = jnp.concatenate([-real_imag[:, width:], real_imag[:, :width]], axis=1)
    return jnp.concatenate([real_imag, swapped], axis=0)


def spectra_kernel(
    dims,
    s_ref,
    high_cos,
    high_sin,
    low_cos,
    low_sin,
    window,
    out_ref,
    table,
    send_buf,
    keep_sem,
    send_sem,
    recv_sem,
):
    freq_devices, src_devices = dims
    devices = freq_devices * src_devices
    my_freq, my_src = lax.axis_index("freq"), lax.axis_index("src")
    slot = my_src * freq_devices + my_freq
    bins = out_ref.shape[2]
    length = s_ref.shape[1]
    members = GROUP_BINS // bins
    groups = devices // members

    def place(index):
        return (lax.rem(index, freq_devices), index // freq_devices)

    barrier = pltpu.get_barrier_semaphore()

    def greet(step, carry):
        pl.semaphore_signal(
            barrier, inc=1, device_id=place(lax.rem(slot + step, devices)), device_id_type=MESH
        )
        return carry

    lax.fori_loop(1, devices, greet, 0)

    def group_of(step):
        return lax.rem(slot // members + step, groups)

    def compute(step):
        group = group_of(step)
        rows = pl.ds(pl.multiple_of(group * GROUP_BINS, GROUP_BINS), GROUP_BINS)
        l_cos, l_sin = low_cos[rows, :], low_sin[rows, :]
        h_cos, h_sin = high_cos[rows, :], high_sin[rows, :]
        for high in range(length // LOW_STEPS):
            columns = slice(high * LOW_STEPS, (high + 1) * LOW_STEPS)
            a_cos, a_sin = h_cos[:, high : high + 1], h_sin[:, high : high + 1]
            weight = window[:, columns]
            table[:GROUP_BINS, columns] = (weight * (a_cos * l_cos - a_sin * l_sin)).astype(
                jnp.bfloat16
            )
            table[GROUP_BINS:, columns] = (-weight * (a_sin * l_cos + a_cos * l_sin)).astype(
                jnp.bfloat16
            )
        y = dot_nt(table[...], s_ref[...]).astype(jnp.bfloat16)
        for member in range(members):
            owner = group * members + member
            send_buf[owner, 0] = y[member * bins : (member + 1) * bins]
            send_buf[owner, 1] = y[GROUP_BINS + member * bins : GROUP_BINS + (member + 1) * bins]

    def send(step):
        for member in range(members):
            owner = group_of(step) * members + lax.rem(slot + member, members)

            @pl.when(owner == slot)
            def _():
                pltpu.make_async_copy(send_buf.at[owner], out_ref.at[slot], keep_sem).start()

            @pl.when(owner != slot)
            def _():
                pltpu.make_async_remote_copy(
                    src_ref=send_buf.at[owner],
                    dst_ref=out_ref.at[slot],
                    send_sem=send_sem,
                    recv_sem=recv_sem,
                    device_id=place(owner),
                    device_id_type=MESH,
                ).start()

    compute(0)
    pl.semaphore_wait(barrier, devices - 1)
    send(0)

    def body(step, carry):
        compute(step)
        send(step)
        return carry

    lax.fori_loop(1, groups, body, 0)
    pltpu.make_async_copy(send_buf.at[slot], out_ref.at[slot], keep_sem).wait()
    others = out_ref.at[pl.ds(0, devices - 1)]
    pltpu.make_async_copy(others, others, send_sem).wait()
    pltpu.make_async_copy(others, others, recv_sem).wait()


def demix_kernel(
    dims,
    x_ref,
    offset_ref,
    out_ref,
    power_ref,
    stage,
    w_buf,
    x_buf,
    y_buf,
    sums,
    power,
    parts,
    received,
    gathered,
    load_sem,
    send_sem,
    recv_sem,
    last_sem,
):
    freq_devices, src_devices, total_bins, frames_here = dims
    devices = freq_devices * src_devices
    my_freq, my_src = lax.axis_index("freq"), lax.axis_index("src")
    me = my_freq * src_devices + my_src
    bins = x_ref.shape[1]
    width = offset_ref.shape[2]
    frames = frames_here * freq_devices
    rows = width // src_devices
    chunk = width // devices

    def place(index):
        return (index // src_devices, lax.rem(index, src_devices))

    load = pltpu.make_async_copy(
        offset_ref.at[:, pl.ds(my_src * bins, bins)], stage, load_sem
    )
    load.start()

    barrier = pltpu.get_barrier_semaphore()

    def greet(step, carry):
        pl.semaphore_signal(
            barrier, inc=1, device_id=place(lax.rem(me + step, devices)), device_id_type=MESH
        )
        return carry

    lax.fori_loop(1, devices, greet, 0)
    load.wait()
    row_id = lax.broadcasted_iota(jnp.int32, (width, 2 * width), 0)
    col_id = lax.broadcasted_iota(jnp.int32, (width, 2 * width), 1)
    identity = jnp.where(row_id == col_id, 1.0, 0.0).astype(jnp.float32)

    def separate(first_bin, w_list, x_list):
        products = []
        for w, x in zip(w_list, x_list):
            high, low = halves(w)
            products.append(dot_nt(jnp.concatenate([high, low], axis=0), x))
        y_list = [(p[:width] + p[width:]).astype(jnp.bfloat16) for p in products]
        squares = 0.0
        for y in y_list:
            values = y.astype(jnp.float32)
            squares = squares + values * values
        for k in range(PAIR):
            w_buf[first_bin + k] = w_list[k]
            y_buf[first_bin + k] = y_list[k]
        sums[...] += squares[:, :frames] + squares[:, frames:]

    def gather_frames(part):
        pieces = [part[k * freq_devices : (k + 1) * freq_devices] for k in range(src_devices)]
        return jnp.concatenate(
            [
                jnp.concatenate([p[:, f * rows : (f + 1) * rows] for p in pieces], axis=1)
                for f in range(frames_here)
            ],
            axis=0,
        )

    def first(step, carry):
        b = step * PAIR
        w_list, x_list = [], []
        for k in range(PAIR):
            w_list.append(jnp.concatenate([stage[0, b + k], stage[1, b + k]], axis=1) + identity)
            x_real, x_imag = gather_frames(x_ref[0, b + k]), gather_frames(x_ref[1, b + k])
            upper = jnp.concatenate([x_real, -x_imag], axis=1)
            lower = jnp.concatenate([x_imag, x_real], axis=1)
            x_list.append(jnp.concatenate([upper, lower], axis=0))
        for k in range(PAIR):
            x_buf[b + k] = x_list[k]
        separate(b, w_list, x_list)
        return carry

    def improved(first_bin, scale):
        y_list = [y_buf[first_bin + k] for k in range(PAIR)]
        w_list = [w_buf[first_bin + k] for k in range(PAIR)]
        diffs = []
        for y in y_list:
            high, low = halves(y.astype(jnp.float32) * scale)
            product = dot_nt(jnp.concatenate([high, low], axis=0), block_pair(y, frames))
            diffs.append(identity - (product[:width] + product[width:]))
        result = []
        for diff, w in zip(diffs, w_list):
            d_high, d_low = halves(diff)
            w_high, w_low = halves(w)
            change = dot_nn(jnp.concatenate([d_high, d_low], axis=0), block_pair(w_high, width))
            change_low = dot_nn(d_high, block_pair(w_low, width))
            result.append(w + step_size * (change[:width] + change[width:] + change_low))
        return result

    def add_up(sweep):
        total = sums[...]
        for owner in range(devices):
            parts[owner] = total[owner * chunk : (owner + 1) * chunk]

        def scatter(step, carry):
            owner = lax.rem(me + step, devices)
            pltpu.make_async_remote_copy(
                src_ref=parts.at[owner],
                dst_ref=received.at[sweep, step - 1],
                send_sem=send_sem.at[sweep, 0],
                recv_sem=recv_sem.at[sweep, 0],
                device_id=place(owner),
                device_id_type=MESH,
            ).start()
            return carry

        lax.fori_loop(1, devices, scatter, 0)
        pltpu.make_async_copy(
            received.at[sweep], received.at[sweep], recv_sem.at[sweep, 0]
        ).wait()
        mine = parts[me] + jnp.sum(received[sweep], axis=0)
        gathered[sweep, me] = jnp.sqrt(mine / total_bins + epsilon)

        def spread(step, carry):
            pltpu.make_async_remote_copy(
                src_ref=gathered.at[sweep, me],
                dst_ref=gathered.at[sweep, me],
                send_sem=send_sem.at[sweep, 1],
                recv_sem=recv_sem.at[sweep, 1],
                device_id=place(lax.rem(me + step, devices)),
                device_id_type=MESH,
            ).start()
            return carry

        lax.fori_loop(1, devices, spread, 0)
        for phase in range(2):
            pltpu.make_async_copy(
                received.at[sweep], received.at[sweep], send_sem.at[sweep, phase]
            ).wait()
        pltpu.make_async_copy(
            received.at[sweep], received.at[sweep], recv_sem.at[sweep, 1]
        ).wait()
        for owner in range(devices):
            power[owner * chunk : (owner + 1) * chunk] = gathered[sweep, owner]
        inverse = 1.0 / (power[...] * frames)
        return jnp.concatenate([inverse, inverse], axis=1)

    sums[...] = jnp.zeros_like(sums)
    lax.fori_loop(0, bins // PAIR, first, 0)
    pl.semaphore_wait(barrier, devices - 1)

    for sweep in range(ITERS - 1):
        scale = add_up(sweep)
        sums[...] = jnp.zeros_like(sums)

        def again(step, carry, scale=scale):
            b = step * PAIR
            x_list = [x_buf[b + k] for k in range(PAIR)]
            separate(b, improved(b, scale), x_list)
            return carry

        lax.fori_loop(0, bins // PAIR, again, 0)

    scale = add_up(ITERS - 1)
    power_ref[...] = power[pl.ds(pl.multiple_of(my_src * rows, rows), rows), :]

    other = 1 - my_src
    own_rows = pl.ds(pl.multiple_of(my_src * rows, rows), rows)
    other_rows = pl.ds(pl.multiple_of(other * rows, rows), rows)

    def keep_copy(start, count):
        return pltpu.make_async_copy(
            stage.at[:, pl.ds(start, count), own_rows],
            out_ref.at[:, pl.ds(my_src * bins + start, count)],
            load_sem,
        )

    def give_copy(start, count):
        return pltpu.make_async_remote_copy(
            src_ref=stage.at[:, pl.ds(start, count), other_rows],
            dst_ref=out_ref.at[:, pl.ds(my_src * bins + start, count)],
            send_sem=last_sem.at[0],
            recv_sem=last_sem.at[1],
            device_id=(my_freq, other),
            device_id_type=MESH,
        )

    def last(step, carry):
        b = step * PAIR
        w_list = improved(b, scale)
        for k in range(PAIR):
            stage[0, b + k] = w_list[k][:, :width]
            stage[1, b + k] = w_list[k][:, width:]
        give_copy(b, PAIR).start()
        keep_copy(b, PAIR).start()
        return carry

    lax.fori_loop(0, bins // PAIR, last, 0)
    keep_copy(0, bins).wait()
    give_copy(0, bins).wait()


def shards(samples, initial_offset):
    freq_devices = lax.axis_size("freq")
    src_devices = lax.axis_size("src")
    devices = freq_devices * src_devices
    frames_here, length, mics_here = samples.shape
    bin_count = length // 2
    pair_bins = initial_offset.shape[1]
    bins = pair_bins // src_devices
    width = initial_offset.shape[2]
    frame_total = frames_here * freq_devices
    chunk = width // devices
    f32, bf16 = jnp.float32, jnp.bfloat16
    row = jnp.arange(bin_count, dtype=jnp.int32)
    bin_idx = (
        row // bins % freq_devices * pair_bins
        + row // (bins * freq_devices) * bins
        + row % bins
    )
    high_cos, high_sin = waves(bin_idx, length // LOW_STEPS, LOW_STEPS, length)
    low_cos, low_sin = waves(bin_idx, LOW_STEPS, 1, length)
    columns = frames_here * mics_here
    frames_of = jnp.transpose(samples, (0, 2, 1)).reshape(columns, length)
    vmem = pl.BlockSpec(memory_space=pltpu.VMEM)
    spectra = pl.pallas_call(
        functools.partial(spectra_kernel, (freq_devices, src_devices)),
        out_shape=jax.ShapeDtypeStruct((devices, 2, bins, columns), bf16),
        in_specs=[vmem] * 6,
        out_specs=vmem,
        scratch_shapes=[
            pltpu.VMEM((2 * GROUP_BINS, length), bf16),
            pltpu.VMEM((devices, 2, bins, columns), bf16),
            pltpu.SemaphoreType.DMA,
            pltpu.SemaphoreType.DMA,
            pltpu.SemaphoreType.DMA,
        ],
        compiler_params=pltpu.CompilerParams(
            collective_id=1, has_side_effects=True, vmem_limit_bytes=40 * 1024 * 1024
        ),
    )(frames_of, high_cos, high_sin, low_cos, low_sin, window_of(length)[None])
    x = jnp.transpose(spectra, (1, 2, 0, 3))
    demixing, power = pl.pallas_call(
        functools.partial(demix_kernel, (freq_devices, src_devices, bin_count, frames_here)),
        out_shape=(
            jax.ShapeDtypeStruct((2, pair_bins, width // src_devices, width), f32),
            jax.ShapeDtypeStruct((width // src_devices, frame_total), f32),
        ),
        in_specs=[
            pl.BlockSpec(memory_space=pltpu.VMEM),
            pl.BlockSpec(memory_space=pl.ANY),
        ],
        out_specs=(
            pl.BlockSpec(memory_space=pl.ANY),
            pl.BlockSpec(memory_space=pltpu.VMEM),
        ),
        scratch_shapes=[
            pltpu.VMEM((2, bins, width, width), f32),
            pltpu.VMEM((bins, width, 2 * width), f32),
            pltpu.VMEM((bins, 2 * frame_total, 2 * width), bf16),
            pltpu.VMEM((bins, width, 2 * frame_total), bf16),
            pltpu.VMEM((width, frame_total), f32),
            pltpu.VMEM((width, frame_total), f32),
            pltpu.VMEM((devices, chunk, frame_total), f32),
            pltpu.VMEM((ITERS, devices - 1, chunk, frame_total), f32),
            pltpu.VMEM((ITERS, devices, chunk, frame_total), f32),
            pltpu.SemaphoreType.DMA,
            pltpu.SemaphoreType.DMA((ITERS, 2)),
            pltpu.SemaphoreType.DMA((ITERS, 2)),
            pltpu.SemaphoreType.DMA((2,)),
        ],
        compiler_params=pltpu.CompilerParams(
            collective_id=0, has_side_effects=True, vmem_limit_bytes=48 * 1024 * 1024
        ),
    )(x, initial_offset)
    power = jnp.transpose(power.reshape(-1, frames_here, freq_devices), (0, 2, 1))
    return demixing, power.reshape(-1, frame_total)


def solution(mesh):
    in_specs = (P("freq", None, "src"), P(None, "freq", None, None))
    out_specs = (P(None, "freq", "src", None), P("src", None))
    return jax.shard_map(shards, mesh=mesh, in_specs=in_specs, out_specs=out_specs, check_vma=False)
```

```python
import functools

import jax
import jax.numpy as jnp
from jax import lax
from jax.experimental import pallas as pl
from jax.experimental.pallas import tpu as pltpu
from jax.sharding import PartitionSpec as P

ITERS = 3

step_size = 0.3
epsilon = 1e-06
MESH = pl.DeviceIdType.MESH
LOW_STEPS = 128
GROUP_BINS = 128
PAIR = 8


def waves(bin_idx, index, length):
    phase = (bin_idx * index % length).astype(jnp.float32) * (
        2.0 * jnp.pi / length
    )
    return jnp.cos(phase), jnp.sin(phase)


def window_of(length):
    sample_idx = jnp.arange(length, dtype=jnp.int32)
    return (
        0.5 - 0.5 * jnp.cos(sample_idx.astype(jnp.float32) * (2.0 * jnp.pi / length))
    ) * jnp.sqrt(jnp.float32(8.0 / (3.0 * length)))


def halves(value):
    high = value.astype(jnp.bfloat16)
    low = (value - high.astype(jnp.float32)).astype(jnp.bfloat16)
    return high, low


def dot_nn(left, right):
    return lax.dot_general(left, right, (((1,), (0,)), ((), ())), preferred_element_type=jnp.float32)


def dot_nt(left, right):
    return lax.dot_general(left, right, (((1,), (1,)), ((), ())), preferred_element_type=jnp.float32)


def block_pair(real_imag, width):
    swapped = jnp.concatenate([-real_imag[:, width:], real_imag[:, :width]], axis=1)
    return jnp.concatenate([real_imag, swapped], axis=0)


def spectra_kernel(
    dims,
    s_ref,
    high_cos,
    high_sin,
    low_cos,
    low_sin,
    window,
    out_ref,
    table,
    send_buf,
    keep_sem,
    send_sem,
    recv_sem,
):
    freq_devices, src_devices = dims
    devices = freq_devices * src_devices
    my_freq, my_src = lax.axis_index("freq"), lax.axis_index("src")
    slot = my_src * freq_devices + my_freq
    bins = out_ref.shape[2]
    length = s_ref.shape[1]
    members = GROUP_BINS // bins
    groups = devices // members

    def place(index):
        return (lax.rem(index, freq_devices), index // freq_devices)

    barrier = pltpu.get_barrier_semaphore()

    def greet(step, carry):
        pl.semaphore_signal(
            barrier, inc=1, device_id=place(lax.rem(slot + step, devices)), device_id_type=MESH
        )
        return carry

    lax.fori_loop(1, devices, greet, 0)

    def group_of(step):
        return lax.rem(slot // members + step + groups // 4, groups)

    def compute(step):
        group = group_of(step)
        rows = pl.ds(pl.multiple_of(group * GROUP_BINS, GROUP_BINS), GROUP_BINS)
        l_cos, l_sin = low_cos[rows, :], low_sin[rows, :]
        h_cos, h_sin = high_cos[:, rows].T, high_sin[:, rows].T
        for high in range(length // LOW_STEPS):
            columns = slice(high * LOW_STEPS, (high + 1) * LOW_STEPS)
            a_cos, a_sin = h_cos[:, high : high + 1], h_sin[:, high : high + 1]
            weight = window[:, columns]
            table[:GROUP_BINS, columns] = (weight * (a_cos * l_cos - a_sin * l_sin)).astype(
                jnp.bfloat16
            )
            table[GROUP_BINS:, columns] = (-weight * (a_sin * l_cos + a_cos * l_sin)).astype(
                jnp.bfloat16
            )
        y = dot_nt(table[...], s_ref[...]).astype(jnp.bfloat16)
        for member in range(members):
            owner = group * members + member
            send_buf[owner, 0] = y[member * bins : (member + 1) * bins]
            send_buf[owner, 1] = y[GROUP_BINS + member * bins : GROUP_BINS + (member + 1) * bins]

    def send(step):
        for member in range(members):
            owner = group_of(step) * members + lax.rem(slot + member, members)

            @pl.when(owner == slot)
            def _():
                pltpu.make_async_copy(send_buf.at[owner], out_ref.at[slot], keep_sem).start()

            @pl.when(owner != slot)
            def _():
                pltpu.make_async_remote_copy(
                    src_ref=send_buf.at[owner],
                    dst_ref=out_ref.at[slot],
                    send_sem=send_sem,
                    recv_sem=recv_sem,
                    device_id=place(owner),
                    device_id_type=MESH,
                ).start()

    compute(0)
    pl.semaphore_wait(barrier, devices - 1)
    send(0)

    def body(step, carry):
        compute(step)
        send(step)
        return carry

    lax.fori_loop(1, groups, body, 0)
    pltpu.make_async_copy(send_buf.at[slot], out_ref.at[slot], keep_sem).wait()
    others = out_ref.at[pl.ds(0, devices - 1)]
    pltpu.make_async_copy(others, others, send_sem).wait()
    pltpu.make_async_copy(others, others, recv_sem).wait()


def demix_kernel(
    dims,
    x_ref,
    offset_ref,
    out_ref,
    power_ref,
    stage,
    w_buf,
    x_buf,
    y_buf,
    sums,
    power,
    parts,
    received,
    gathered,
    load_sem,
    send_sem,
    recv_sem,
    last_sem,
):
    freq_devices, src_devices, total_bins, frames_here = dims
    devices = freq_devices * src_devices
    my_freq, my_src = lax.axis_index("freq"), lax.axis_index("src")
    me = my_freq * src_devices + my_src
    bins = x_ref.shape[1]
    width = offset_ref.shape[2]
    frames = frames_here * freq_devices
    rows = width // src_devices
    chunk = width // devices

    def place(index):
        return (index // src_devices, lax.rem(index, src_devices))

    load = pltpu.make_async_copy(
        offset_ref.at[:, pl.ds(my_src * bins, bins)], stage, load_sem
    )
    load.start()

    barrier = pltpu.get_barrier_semaphore()

    def greet(step, carry):
        pl.semaphore_signal(
            barrier, inc=1, device_id=place(lax.rem(me + step, devices)), device_id_type=MESH
        )
        return carry

    lax.fori_loop(1, devices, greet, 0)
    load.wait()
    row_id = lax.broadcasted_iota(jnp.int32, (width, 2 * width), 0)
    col_id = lax.broadcasted_iota(jnp.int32, (width, 2 * width), 1)
    identity = jnp.where(row_id == col_id, 1.0, 0.0).astype(jnp.float32)

    def separate(first_bin, w_list, x_list):
        products = []
        for w, x in zip(w_list, x_list):
            high, low = halves(w)
            products.append(dot_nt(jnp.concatenate([high, low], axis=0), x))
        y_list = [(p[:width] + p[width:]).astype(jnp.bfloat16) for p in products]
        squares = 0.0
        for y in y_list:
            values = y.astype(jnp.float32)
            squares = squares + values * values
        for k in range(PAIR):
            w_buf[first_bin + k] = w_list[k]
            y_buf[first_bin + k] = y_list[k]
        sums[...] += squares[:, :frames] + squares[:, frames:]

    def gather_frames(part):
        pieces = [part[k * freq_devices : (k + 1) * freq_devices] for k in range(src_devices)]
        return jnp.concatenate(
            [
                jnp.concatenate([p[:, f * rows : (f + 1) * rows] for p in pieces], axis=1)
                for f in range(frames_here)
            ],
            axis=0,
        )

    def first(step, carry):
        b = step * PAIR
        w_list, x_list = [], []
        for k in range(PAIR):
            w_list.append(jnp.concatenate([stage[0, b + k], stage[1, b + k]], axis=1) + identity)
            x_real, x_imag = gather_frames(x_ref[0, b + k]), gather_frames(x_ref[1, b + k])
            upper = jnp.concatenate([x_real, -x_imag], axis=1)
            lower = jnp.concatenate([x_imag, x_real], axis=1)
            x_list.append(jnp.concatenate([upper, lower], axis=0))
        for k in range(PAIR):
            x_buf[b + k] = x_list[k]
        separate(b, w_list, x_list)
        return carry

    def improved(first_bin, scale):
        y_list = [y_buf[first_bin + k] for k in range(PAIR)]
        w_list = [w_buf[first_bin + k] for k in range(PAIR)]
        diffs = []
        for y in y_list:
            high, low = halves(y.astype(jnp.float32) * scale)
            product = dot_nt(jnp.concatenate([high, low], axis=0), block_pair(y, frames))
            diffs.append(identity - (product[:width] + product[width:]))
        result = []
        for diff, w in zip(diffs, w_list):
            d_high, d_low = halves(diff)
            w_high, w_low = halves(w)
            change = dot_nn(jnp.concatenate([d_high, d_low], axis=0), block_pair(w_high, width))
            change_low = dot_nn(d_high, block_pair(w_low, width))
            result.append(w + step_size * (change[:width] + change[width:] + change_low))
        return result

    def add_up(sweep):
        total = sums[...]
        for owner in range(devices):
            parts[owner] = total[owner * chunk : (owner + 1) * chunk]

        def scatter(step, carry):
            owner = lax.rem(me + step, devices)
            pltpu.make_async_remote_copy(
                src_ref=parts.at[owner],
                dst_ref=received.at[sweep, step - 1],
                send_sem=send_sem.at[sweep, 0],
                recv_sem=recv_sem.at[sweep, 0],
                device_id=place(owner),
                device_id_type=MESH,
            ).start()
            return carry

        lax.fori_loop(1, devices, scatter, 0)
        pltpu.make_async_copy(
            received.at[sweep], received.at[sweep], recv_sem.at[sweep, 0]
        ).wait()
        mine = parts[me] + jnp.sum(received[sweep], axis=0)
        gathered[sweep, me] = jnp.sqrt(mine / total_bins + epsilon)

        def spread(step, carry):
            pltpu.make_async_remote_copy(
                src_ref=gathered.at[sweep, me],
                dst_ref=gathered.at[sweep, me],
                send_sem=send_sem.at[sweep, 1],
                recv_sem=recv_sem.at[sweep, 1],
                device_id=place(lax.rem(me + step, devices)),
                device_id_type=MESH,
            ).start()
            return carry

        lax.fori_loop(1, devices, spread, 0)
        for phase in range(2):
            pltpu.make_async_copy(
                received.at[sweep], received.at[sweep], send_sem.at[sweep, phase]
            ).wait()
        pltpu.make_async_copy(
            received.at[sweep], received.at[sweep], recv_sem.at[sweep, 1]
        ).wait()
        for owner in range(devices):
            power[owner * chunk : (owner + 1) * chunk] = gathered[sweep, owner]
        inverse = 1.0 / (power[...] * frames)
        return jnp.concatenate([inverse, inverse], axis=1)

    sums[...] = jnp.zeros_like(sums)
    lax.fori_loop(0, bins // PAIR, first, 0)
    pl.semaphore_wait(barrier, devices - 1)

    for sweep in range(ITERS - 1):
        scale = add_up(sweep)
        sums[...] = jnp.zeros_like(sums)

        def again(step, carry, scale=scale):
            b = step * PAIR
            x_list = [x_buf[b + k] for k in range(PAIR)]
            separate(b, improved(b, scale), x_list)
            return carry

        lax.fori_loop(0, bins // PAIR, again, 0)

    scale = add_up(ITERS - 1)
    power_ref[...] = power[pl.ds(pl.multiple_of(my_src * rows, rows), rows), :]

    other = 1 - my_src
    own_rows = pl.ds(pl.multiple_of(my_src * rows, rows), rows)
    other_rows = pl.ds(pl.multiple_of(other * rows, rows), rows)

    def keep_copy(start, count):
        return pltpu.make_async_copy(
            stage.at[:, pl.ds(start, count), own_rows],
            out_ref.at[:, pl.ds(my_src * bins + start, count)],
            load_sem,
        )

    def give_copy(start, count):
        return pltpu.make_async_remote_copy(
            src_ref=stage.at[:, pl.ds(start, count), other_rows],
            dst_ref=out_ref.at[:, pl.ds(my_src * bins + start, count)],
            send_sem=last_sem.at[0],
            recv_sem=last_sem.at[1],
            device_id=(my_freq, other),
            device_id_type=MESH,
        )

    def last(step, carry):
        b = step * PAIR
        w_list = improved(b, scale)
        for k in range(PAIR):
            stage[0, b + k] = w_list[k][:, :width]
            stage[1, b + k] = w_list[k][:, width:]
        give_copy(b, PAIR).start()
        keep_copy(b, PAIR).start()
        return carry

    lax.fori_loop(0, bins // PAIR, last, 0)
    keep_copy(0, bins).wait()
    give_copy(0, bins).wait()


def shards(samples, initial_offset):
    freq_devices = lax.axis_size("freq")
    src_devices = lax.axis_size("src")
    devices = freq_devices * src_devices
    frames_here, length, mics_here = samples.shape
    bin_count = length // 2
    pair_bins = initial_offset.shape[1]
    bins = pair_bins // src_devices
    width = initial_offset.shape[2]
    frame_total = frames_here * freq_devices
    chunk = width // devices
    f32, bf16 = jnp.float32, jnp.bfloat16
    row = jnp.arange(bin_count, dtype=jnp.int32)
    bin_idx = (
        row // bins % freq_devices * pair_bins
        + row // (bins * freq_devices) * bins
        + row % bins
    )
    high = jnp.arange(length // LOW_STEPS, dtype=jnp.int32) * LOW_STEPS
    low = jnp.arange(LOW_STEPS, dtype=jnp.int32)
    high_cos, high_sin = waves(bin_idx[None, :], high[:, None], length)
    low_cos, low_sin = waves(bin_idx[:, None], low[None, :], length)
    columns = frames_here * mics_here
    frames_of = jnp.transpose(samples, (0, 2, 1)).reshape(columns, length)
    vmem = pl.BlockSpec(memory_space=pltpu.VMEM)
    spectra = pl.pallas_call(
        functools.partial(spectra_kernel, (freq_devices, src_devices)),
        out_shape=jax.ShapeDtypeStruct((devices, 2, bins, columns), bf16),
        in_specs=[vmem] * 6,
        out_specs=vmem,
        scratch_shapes=[
            pltpu.VMEM((2 * GROUP_BINS, length), bf16),
            pltpu.VMEM((devices, 2, bins, columns), bf16),
            pltpu.SemaphoreType.DMA,
            pltpu.SemaphoreType.DMA,
            pltpu.SemaphoreType.DMA,
        ],
        compiler_params=pltpu.CompilerParams(
            collective_id=1, has_side_effects=True, vmem_limit_bytes=40 * 1024 * 1024
        ),
    )(frames_of, high_cos, high_sin, low_cos, low_sin, window_of(length)[None])
    x = jnp.transpose(spectra, (1, 2, 0, 3))
    demixing, power = pl.pallas_call(
        functools.partial(demix_kernel, (freq_devices, src_devices, bin_count, frames_here)),
        out_shape=(
            jax.ShapeDtypeStruct((2, pair_bins, width // src_devices, width), f32),
            jax.ShapeDtypeStruct((width // src_devices, frame_total), f32),
        ),
        in_specs=[
            pl.BlockSpec(memory_space=pltpu.VMEM),
            pl.BlockSpec(memory_space=pl.ANY),
        ],
        out_specs=(
            pl.BlockSpec(memory_space=pl.ANY),
            pl.BlockSpec(memory_space=pltpu.VMEM),
        ),
        scratch_shapes=[
            pltpu.VMEM((2, bins, width, width), f32),
            pltpu.VMEM((bins, width, 2 * width), f32),
            pltpu.VMEM((bins, 2 * frame_total, 2 * width), bf16),
            pltpu.VMEM((bins, width, 2 * frame_total), bf16),
            pltpu.VMEM((width, frame_total), f32),
            pltpu.VMEM((width, frame_total), f32),
            pltpu.VMEM((devices, chunk, frame_total), f32),
            pltpu.VMEM((ITERS, devices - 1, chunk, frame_total), f32),
            pltpu.VMEM((ITERS, devices, chunk, frame_total), f32),
            pltpu.SemaphoreType.DMA,
            pltpu.SemaphoreType.DMA((ITERS, 2)),
            pltpu.SemaphoreType.DMA((ITERS, 2)),
            pltpu.SemaphoreType.DMA((2,)),
        ],
        compiler_params=pltpu.CompilerParams(
            collective_id=0, has_side_effects=True, vmem_limit_bytes=48 * 1024 * 1024
        ),
    )(x, initial_offset)
    power = jnp.transpose(power.reshape(-1, frames_here, freq_devices), (0, 2, 1))
    return demixing, power.reshape(-1, frame_total)


def solution(mesh):
    in_specs = (P("freq", None, "src"), P(None, "freq", None, None))
    out_specs = (P(None, "freq", "src", None), P("src", None))
    return jax.shard_map(shards, mesh=mesh, in_specs=in_specs, out_specs=out_specs, check_vma=False)
```

```python
import functools

import jax
import jax.numpy as jnp
from jax import lax
from jax.experimental import pallas as pl
from jax.experimental.pallas import tpu as pltpu
from jax.sharding import PartitionSpec as P

ITERS = 3

step_size = 0.3
epsilon = 1e-06
MESH = pl.DeviceIdType.MESH
LOW_STEPS = 128
GROUP_BINS = 128
BATCH = 16


def waves(bin_idx, index, length):
    phase = (bin_idx * index % length).astype(jnp.float32) * (
        2.0 * jnp.pi / length
    )
    return jnp.cos(phase), jnp.sin(phase)


def window_of(length):
    sample_idx = jnp.arange(length, dtype=jnp.int32)
    return (
        0.5 - 0.5 * jnp.cos(sample_idx.astype(jnp.float32) * (2.0 * jnp.pi / length))
    ) * jnp.sqrt(jnp.float32(8.0 / (3.0 * length)))


def halves(value):
    high = value.astype(jnp.bfloat16)
    low = (value - high.astype(jnp.float32)).astype(jnp.bfloat16)
    return high, low


def dot_nn(left, right):
    return lax.dot_general(left, right, (((1,), (0,)), ((), ())), preferred_element_type=jnp.float32)


def dot_nt(left, right):
    return lax.dot_general(left, right, (((1,), (1,)), ((), ())), preferred_element_type=jnp.float32)


def block_pair(real_imag, width):
    swapped = jnp.concatenate([-real_imag[:, width:], real_imag[:, :width]], axis=1)
    return jnp.concatenate([real_imag, swapped], axis=0)


def spectra_kernel(
    dims,
    s_ref,
    high_cos,
    high_sin,
    low_cos,
    low_sin,
    window,
    out_ref,
    table,
    send_buf,
    keep_sem,
    send_sem,
    recv_sem,
):
    freq_devices, src_devices = dims
    devices = freq_devices * src_devices
    my_freq, my_src = lax.axis_index("freq"), lax.axis_index("src")
    slot = my_src * freq_devices + my_freq
    bins = out_ref.shape[2]
    length = s_ref.shape[1]
    members = GROUP_BINS // bins
    groups = devices // members

    def place(index):
        return (lax.rem(index, freq_devices), index // freq_devices)

    barrier = pltpu.get_barrier_semaphore()

    def greet(step, carry):
        pl.semaphore_signal(
            barrier, inc=1, device_id=place(lax.rem(slot + step, devices)), device_id_type=MESH
        )
        return carry

    lax.fori_loop(1, devices, greet, 0)

    def group_of(step):
        return lax.rem(slot // members + step + groups // 4, groups)

    def compute(step):
        group = group_of(step)
        rows = pl.ds(pl.multiple_of(group * GROUP_BINS, GROUP_BINS), GROUP_BINS)
        l_cos, l_sin = low_cos[rows, :], low_sin[rows, :]
        h_cos, h_sin = high_cos[:, rows].T, high_sin[:, rows].T
        for high in range(length // LOW_STEPS):
            columns = slice(high * LOW_STEPS, (high + 1) * LOW_STEPS)
            a_cos, a_sin = h_cos[:, high : high + 1], h_sin[:, high : high + 1]
            weight = window[:, columns]
            table[:GROUP_BINS, columns] = (weight * (a_cos * l_cos - a_sin * l_sin)).astype(
                jnp.bfloat16
            )
            table[GROUP_BINS:, columns] = (-weight * (a_sin * l_cos + a_cos * l_sin)).astype(
                jnp.bfloat16
            )
        y = dot_nt(table[...], s_ref[...]).astype(jnp.bfloat16)
        for member in range(members):
            owner = group * members + member
            send_buf[owner, 0] = y[member * bins : (member + 1) * bins]
            send_buf[owner, 1] = y[GROUP_BINS + member * bins : GROUP_BINS + (member + 1) * bins]

    def send(step):
        for member in range(members):
            owner = group_of(step) * members + lax.rem(slot + member, members)

            @pl.when(owner == slot)
            def _():
                pltpu.make_async_copy(send_buf.at[owner], out_ref.at[slot], keep_sem).start()

            @pl.when(owner != slot)
            def _():
                pltpu.make_async_remote_copy(
                    src_ref=send_buf.at[owner],
                    dst_ref=out_ref.at[slot],
                    send_sem=send_sem,
                    recv_sem=recv_sem,
                    device_id=place(owner),
                    device_id_type=MESH,
                ).start()

    compute(0)
    pl.semaphore_wait(barrier, devices - 1)
    send(0)

    def body(step, carry):
        compute(step)
        send(step)
        return carry

    lax.fori_loop(1, groups, body, 0)
    pltpu.make_async_copy(send_buf.at[slot], out_ref.at[slot], keep_sem).wait()
    others = out_ref.at[pl.ds(0, devices - 1)]
    pltpu.make_async_copy(others, others, send_sem).wait()
    pltpu.make_async_copy(others, others, recv_sem).wait()


def demix_kernel(
    dims,
    x_ref,
    offset_ref,
    out_ref,
    power_ref,
    stage,
    w_buf,
    x_buf,
    y_buf,
    sums,
    power,
    parts,
    received,
    gathered,
    load_sem,
    send_sem,
    recv_sem,
    last_sem,
):
    freq_devices, src_devices, total_bins, frames_here = dims
    devices = freq_devices * src_devices
    my_freq, my_src = lax.axis_index("freq"), lax.axis_index("src")
    me = my_freq * src_devices + my_src
    bins = x_ref.shape[1]
    width = offset_ref.shape[2]
    frames = frames_here * freq_devices
    rows = width // src_devices
    batch = min(BATCH, bins)
    chunk = width // devices

    def place(index):
        return (index // src_devices, lax.rem(index, src_devices))

    load = pltpu.make_async_copy(
        offset_ref.at[:, pl.ds(my_src * bins, bins)], stage, load_sem
    )
    load.start()

    barrier = pltpu.get_barrier_semaphore()

    def greet(step, carry):
        pl.semaphore_signal(
            barrier, inc=1, device_id=place(lax.rem(me + step, devices)), device_id_type=MESH
        )
        return carry

    lax.fori_loop(1, devices, greet, 0)
    load.wait()
    row_id = lax.broadcasted_iota(jnp.int32, (width, 2 * width), 0)
    col_id = lax.broadcasted_iota(jnp.int32, (width, 2 * width), 1)
    identity = jnp.where(row_id == col_id, 1.0, 0.0).astype(jnp.float32)

    def separate(first_bin, w_list, x_list):
        products = []
        for w, x in zip(w_list, x_list):
            high, low = halves(w)
            products.append(dot_nt(jnp.concatenate([high, low], axis=0), x))
        y_list = [(p[:width] + p[width:]).astype(jnp.bfloat16) for p in products]
        squares = 0.0
        for y in y_list:
            values = y.astype(jnp.float32)
            squares = squares + values * values
        for k in range(batch):
            w_buf[first_bin + k] = w_list[k]
            y_buf[first_bin + k] = y_list[k]
        sums[...] += squares[:, :frames] + squares[:, frames:]

    def gather_frames(part):
        pieces = [part[k * freq_devices : (k + 1) * freq_devices] for k in range(src_devices)]
        return jnp.concatenate(
            [
                jnp.concatenate([p[:, f * rows : (f + 1) * rows] for p in pieces], axis=1)
                for f in range(frames_here)
            ],
            axis=0,
        )

    def first(step, carry):
        b = step * batch
        w_list, x_list = [], []
        for k in range(batch):
            w_list.append(jnp.concatenate([stage[0, b + k], stage[1, b + k]], axis=1) + identity)
            x_real, x_imag = gather_frames(x_ref[0, b + k]), gather_frames(x_ref[1, b + k])
            upper = jnp.concatenate([x_real, -x_imag], axis=1)
            lower = jnp.concatenate([x_imag, x_real], axis=1)
            x_list.append(jnp.concatenate([upper, lower], axis=0))
        for k in range(batch):
            x_buf[b + k] = x_list[k]
        separate(b, w_list, x_list)
        return carry

    def improved(first_bin, scale):
        y_list = [y_buf[first_bin + k] for k in range(batch)]
        w_list = [w_buf[first_bin + k] for k in range(batch)]
        diffs = []
        for y in y_list:
            high, low = halves(y.astype(jnp.float32) * scale)
            product = dot_nt(jnp.concatenate([high, low], axis=0), block_pair(y, frames))
            diffs.append(identity - (product[:width] + product[width:]))
        result = []
        for diff, w in zip(diffs, w_list):
            d_high, d_low = halves(diff)
            w_high, w_low = halves(w)
            change = dot_nn(jnp.concatenate([d_high, d_low], axis=0), block_pair(w_high, width))
            change_low = dot_nn(d_high, block_pair(w_low, width))
            result.append(w + step_size * (change[:width] + change[width:] + change_low))
        return result

    def add_up(sweep):
        total = sums[...]
        for owner in range(devices):
            parts[owner] = total[owner * chunk : (owner + 1) * chunk]

        def scatter(step, carry):
            owner = lax.rem(me + step, devices)
            pltpu.make_async_remote_copy(
                src_ref=parts.at[owner],
                dst_ref=received.at[sweep, step - 1],
                send_sem=send_sem.at[sweep, 0],
                recv_sem=recv_sem.at[sweep, 0],
                device_id=place(owner),
                device_id_type=MESH,
            ).start()
            return carry

        lax.fori_loop(1, devices, scatter, 0)
        pltpu.make_async_copy(
            received.at[sweep], received.at[sweep], recv_sem.at[sweep, 0]
        ).wait()
        mine = parts[me] + jnp.sum(received[sweep], axis=0)
        gathered[sweep, me] = jnp.sqrt(mine / total_bins + epsilon)

        def spread(step, carry):
            pltpu.make_async_remote_copy(
                src_ref=gathered.at[sweep, me],
                dst_ref=gathered.at[sweep, me],
                send_sem=send_sem.at[sweep, 1],
                recv_sem=recv_sem.at[sweep, 1],
                device_id=place(lax.rem(me + step, devices)),
                device_id_type=MESH,
            ).start()
            return carry

        lax.fori_loop(1, devices, spread, 0)
        for phase in range(2):
            pltpu.make_async_copy(
                received.at[sweep], received.at[sweep], send_sem.at[sweep, phase]
            ).wait()
        pltpu.make_async_copy(
            received.at[sweep], received.at[sweep], recv_sem.at[sweep, 1]
        ).wait()
        for owner in range(devices):
            power[owner * chunk : (owner + 1) * chunk] = gathered[sweep, owner]
        inverse = 1.0 / (power[...] * frames)
        return jnp.concatenate([inverse, inverse], axis=1)

    sums[...] = jnp.zeros_like(sums)
    lax.fori_loop(0, bins // batch, first, 0)
    pl.semaphore_wait(barrier, devices - 1)

    for sweep in range(ITERS - 1):
        scale = add_up(sweep)
        sums[...] = jnp.zeros_like(sums)

        def again(step, carry, scale=scale):
            b = step * batch
            x_list = [x_buf[b + k] for k in range(batch)]
            separate(b, improved(b, scale), x_list)
            return carry

        lax.fori_loop(0, bins // batch, again, 0)

    scale = add_up(ITERS - 1)
    power_ref[...] = power[pl.ds(pl.multiple_of(my_src * rows, rows), rows), :]

    other = 1 - my_src
    own_rows = pl.ds(pl.multiple_of(my_src * rows, rows), rows)
    other_rows = pl.ds(pl.multiple_of(other * rows, rows), rows)

    def keep_copy(start, count):
        return pltpu.make_async_copy(
            stage.at[:, pl.ds(start, count), own_rows],
            out_ref.at[:, pl.ds(my_src * bins + start, count)],
            load_sem,
        )

    def give_copy(start, count):
        return pltpu.make_async_remote_copy(
            src_ref=stage.at[:, pl.ds(start, count), other_rows],
            dst_ref=out_ref.at[:, pl.ds(my_src * bins + start, count)],
            send_sem=last_sem.at[0],
            recv_sem=last_sem.at[1],
            device_id=(my_freq, other),
            device_id_type=MESH,
        )

    def last(step, carry):
        b = step * batch
        w_list = improved(b, scale)
        for k in range(batch):
            stage[0, b + k] = w_list[k][:, :width]
            stage[1, b + k] = w_list[k][:, width:]
        give_copy(b, batch).start()
        keep_copy(b, batch).start()
        return carry

    lax.fori_loop(0, bins // batch, last, 0)
    keep_copy(0, bins).wait()
    give_copy(0, bins).wait()


def shards(samples, initial_offset):
    freq_devices = lax.axis_size("freq")
    src_devices = lax.axis_size("src")
    devices = freq_devices * src_devices
    frames_here, length, mics_here = samples.shape
    bin_count = length // 2
    pair_bins = initial_offset.shape[1]
    bins = pair_bins // src_devices
    width = initial_offset.shape[2]
    frame_total = frames_here * freq_devices
    chunk = width // devices
    f32, bf16 = jnp.float32, jnp.bfloat16
    row = jnp.arange(bin_count, dtype=jnp.int32)
    bin_idx = (
        row // bins % freq_devices * pair_bins
        + row // (bins * freq_devices) * bins
        + row % bins
    )
    high = jnp.arange(length // LOW_STEPS, dtype=jnp.int32) * LOW_STEPS
    low = jnp.arange(LOW_STEPS, dtype=jnp.int32)
    high_cos, high_sin = waves(bin_idx[None, :], high[:, None], length)
    low_cos, low_sin = waves(bin_idx[:, None], low[None, :], length)
    columns = frames_here * mics_here
    frames_of = jnp.transpose(samples, (0, 2, 1)).reshape(columns, length)
    vmem = pl.BlockSpec(memory_space=pltpu.VMEM)
    spectra = pl.pallas_call(
        functools.partial(spectra_kernel, (freq_devices, src_devices)),
        out_shape=jax.ShapeDtypeStruct((devices, 2, bins, columns), bf16),
        in_specs=[vmem] * 6,
        out_specs=vmem,
        scratch_shapes=[
            pltpu.VMEM((2 * GROUP_BINS, length), bf16),
            pltpu.VMEM((devices, 2, bins, columns), bf16),
            pltpu.SemaphoreType.DMA,
            pltpu.SemaphoreType.DMA,
            pltpu.SemaphoreType.DMA,
        ],
        compiler_params=pltpu.CompilerParams(
            collective_id=1, has_side_effects=True, vmem_limit_bytes=40 * 1024 * 1024
        ),
    )(frames_of, high_cos, high_sin, low_cos, low_sin, window_of(length)[None])
    x = jnp.transpose(spectra, (1, 2, 0, 3))
    demixing, power = pl.pallas_call(
        functools.partial(demix_kernel, (freq_devices, src_devices, bin_count, frames_here)),
        out_shape=(
            jax.ShapeDtypeStruct((2, pair_bins, width // src_devices, width), f32),
            jax.ShapeDtypeStruct((width // src_devices, frame_total), f32),
        ),
        in_specs=[
            pl.BlockSpec(memory_space=pltpu.VMEM),
            pl.BlockSpec(memory_space=pl.ANY),
        ],
        out_specs=(
            pl.BlockSpec(memory_space=pl.ANY),
            pl.BlockSpec(memory_space=pltpu.VMEM),
        ),
        scratch_shapes=[
            pltpu.VMEM((2, bins, width, width), f32),
            pltpu.VMEM((bins, width, 2 * width), f32),
            pltpu.VMEM((bins, 2 * frame_total, 2 * width), bf16),
            pltpu.VMEM((bins, width, 2 * frame_total), bf16),
            pltpu.VMEM((width, frame_total), f32),
            pltpu.VMEM((width, frame_total), f32),
            pltpu.VMEM((devices, chunk, frame_total), f32),
            pltpu.VMEM((ITERS, devices - 1, chunk, frame_total), f32),
            pltpu.VMEM((ITERS, devices, chunk, frame_total), f32),
            pltpu.SemaphoreType.DMA,
            pltpu.SemaphoreType.DMA((ITERS, 2)),
            pltpu.SemaphoreType.DMA((ITERS, 2)),
            pltpu.SemaphoreType.DMA((2,)),
        ],
        compiler_params=pltpu.CompilerParams(
            collective_id=0, has_side_effects=True, vmem_limit_bytes=48 * 1024 * 1024
        ),
    )(x, initial_offset)
    power = jnp.transpose(power.reshape(-1, frames_here, freq_devices), (0, 2, 1))
    return demixing, power.reshape(-1, frame_total)


def solution(mesh):
    in_specs = (P("freq", None, "src"), P(None, "freq", None, None))
    out_specs = (P(None, "freq", "src", None), P("src", None))
    return jax.shard_map(shards, mesh=mesh, in_specs=in_specs, out_specs=out_specs, check_vma=False)
```
